128 devices in a mesh: az: 8 (over x_hi, z), acq: 16 (over x_lo, y, core).
Axes of the slice: x: 4 (x_hi: 2, x_lo: 2; x = x_hi * 2 + x_lo), y: 4, z: 4, core: 2. Of those that a mesh axis runs over, the one named last changes fastest.
Arguments:
- radar_stack: bfloat16 [2, 64, 8192, 256], P(None, 'acq', 'az'), may hold values from -8 to 8
- band_taps: bfloat16 [2, 64, 127], P(None, 'acq'), may hold values from -0.375 to 0.375
- pair_list: int32 [256, 2], replicated, may hold values from 0 to 63, as said below
Outputs:
- acquisition_phase: float32 [64, 131072], P(None, ('az', 'acq'))
The draws below stay inside these ranges and needn't reach their ends.
Inputs may be any that keep to these rules, and one draw needn't show every extreme that they name: `pair_list`: row p has reference p // 4. Cut the acquisitions into as many consecutive equal groups as the acq axis has devices, closed into a cycle: the 4 secondaries of one reference lie one in each of the 4 groups that follow the reference's group on the cycle, in an order drawn anew for every reference.
All inputs are finite; a program needn't handle non-finite values.
Results may differ from the reference program's by a relative error of at most 0.0046.
Values may be sent and summed in bfloat16 or wider, within the bound.
No kernel may reach another device: no remote copies, remote signals or barrier semaphores. Data moves between devices by JAX's collectives and lax.ppermute only.
A program may use at most 128 MiB of HBM per device.

```python
import jax
import jax.numpy as jnp
from jax import lax

ACQ = 64
RG = 256
ROWS_DEV = 1024
HALF = 63
LOOK = 4
REACH = 4
TAPS = 127
AZ = 8192
N_ACQ = 16


def draw_pair_list(key, part):
    local_count = ACQ // N_ACQ
    key_order, key_slot = jax.random.split(jax.random.fold_in(key, 17))
    scores = jax.random.randint(key_order, (ACQ, REACH), 0, 1 << 20) * REACH + jnp.arange(REACH, dtype=jnp.int32)
    order = jnp.argsort(scores, axis=1, stable=True).astype(jnp.int32)
    slots = jax.random.randint(key_slot, (ACQ, REACH), 0, local_count)
    first = jnp.arange(ACQ, dtype=jnp.int32)[:, None] + jnp.zeros((1, REACH), jnp.int32)
    group = first // local_count
    second = (group + order + 1) % N_ACQ * local_count + slots
    return jnp.stack([first, second], axis=-1).reshape(ACQ * REACH, 2).astype(jnp.int32)


def steps_of(own_key, dims, cuts, low, largest):
    factor_of, own = 1.0, jax.random.fold_in(own_key, 6)
    for axis_at, shards_of in cuts:
        draws = jnp.exp(jax.random.uniform(jax.random.fold_in(own, axis_at), (shards_of,), jnp.float32, low / len(cuts), largest / len(cuts)))
        factor_of = factor_of * jnp.repeat(draws, dims[axis_at] // shards_of).reshape([-1 if axis == axis_at else 1 for axis in range(len(dims))])
    return factor_of


def scatter_about(own_key, dims, scale, bound, cuts=(), kind=jnp.bfloat16):
    level = steps_of(own_key, dims, cuts, -0.22, 0.18) if cuts else 1.0
    array = jax.random.normal(own_key, dims, jnp.float32) * scale * level
    return jnp.minimum(jnp.maximum(array, -bound), bound).astype(kind)


def setup_inputs(seed: int = 0) -> dict:
    key_list = jax.random.split(jax.random.key(seed), 4)
    radar_stack = scatter_about(key_list[0], (2, ACQ, AZ, RG), 1.5, 8.0, ((1, 16), (2, 8)))
    band_taps = scatter_about(key_list[1], (2, ACQ, TAPS), (2 * TAPS) ** -0.5, 0.375, ((1, 16),))
    pair_list = draw_pair_list(jax.random.fold_in(key_list[3], 71), 0)
    return dict(radar_stack=radar_stack, band_taps=band_taps, pair_list=pair_list)


ridge_weight = 1.0

def band_matrix(taps, rows):
    width = rows + taps.shape[-1] - 1
    lead = taps.shape[:-1]
    line = jnp.concatenate([taps, jnp.zeros(lead + (rows,), taps.dtype)], axis=-1)
    tiled = jnp.tile(line, (1,) * len(lead) + (rows,))
    return tiled[..., :rows * width].reshape(lead + (rows, width))

def matmul(left, right):
    return jnp.dot(left.astype(jnp.float32), right.astype(jnp.float32), precision=lax.Precision.HIGHEST, preferred_element_type=jnp.float32)

def filter_one(pieces):
    taps_one, image = pieces
    padded = jnp.pad(image, ((0, 0), (HALF, HALF), (0, 0)))
    matrix = band_matrix(taps_one, ROWS_DEV).astype(jnp.float32)
    blocks = AZ // ROWS_DEV

    def one_block(index):
        piece = lax.dynamic_slice_in_dim(padded, index * ROWS_DEV, ROWS_DEV + 2 * HALF, 1).astype(jnp.float32)
        real = matmul(matrix[0], piece[0]) - matmul(matrix[1], piece[1])
        imag = matmul(matrix[0], piece[1]) + matmul(matrix[1], piece[0])
        return jnp.stack([real, imag]).astype(jnp.bfloat16)
    out = lax.map(one_block, jnp.arange(blocks, dtype=jnp.int32))
    return out.transpose(1, 0, 2, 3).reshape(2, AZ, RG)

def reference(radar_stack, band_taps, pair_list):
    filtered = lax.map(filter_one, (band_taps.transpose(1, 0, 2), radar_stack.transpose(1, 0, 2, 3)))
    filtered = filtered.transpose(1, 0, 2, 3)

    def one_pair(pair):
        first = lax.dynamic_index_in_dim(filtered, pair[0], 1, keepdims=False).astype(jnp.float32)
        second = lax.dynamic_index_in_dim(filtered, pair[1], 1, keepdims=False).astype(jnp.float32)
        real = first[0] * second[0] + first[1] * second[1]
        imag = first[1] * second[0] - first[0] * second[1]
        real = real.reshape(AZ // LOOK, LOOK, RG // LOOK, LOOK).sum(axis=(1, 3)) / (LOOK * LOOK)
        imag = imag.reshape(AZ // LOOK, LOOK, RG // LOOK, LOOK).sum(axis=(1, 3)) / (LOOK * LOOK)
        magnitude = jnp.sqrt(real * real + imag * imag)
        return (imag / jnp.maximum(magnitude, 1.0)).reshape(-1)
    phase_lin = lax.map(one_pair, pair_list)
    labels = jnp.arange(ACQ, dtype=jnp.int32)
    incidence = (pair_list[:, 1:2] == labels).astype(jnp.float32) - (pair_list[:, 0:1] == labels).astype(jnp.float32)
    normal = matmul(incidence.T, incidence) + ridge_weight * jnp.eye(ACQ, dtype=jnp.float32)
    inverse_map = jnp.linalg.solve(normal, incidence.T)
    return matmul(inverse_map, phase_lin)
```

```python
import jax
import jax.numpy as jnp
from jax import lax
from jax.experimental import pallas as pl
from jax.experimental.pallas import tpu as pltpu
from jax.sharding import PartitionSpec as P

LOOK = 4
REACH = 4
BLOCK = 128
CHUNK = 64
HALO = 64
RIDGE = 1.0
MIB = 1 << 20


def column_order(columns):
    source = lax.broadcasted_iota(jnp.int32, (columns, columns), 0)
    target = lax.broadcasted_iota(jnp.int32, (columns, columns), 1)
    looked = columns // LOOK
    wanted = (target % looked) * LOOK + target // looked
    return jnp.where(source == wanted, 1.0, 0.0).astype(jnp.bfloat16)


def fill_bands(taps_ref, band_ref, a):
    lines = [jnp.broadcast_to(taps_ref[part, a : a + 1, :], (8, 2 * BLOCK)) for part in range(2)]
    for m in range(0, BLOCK, 16):
        chunk, look = m // CHUNK, m % CHUNK // 16
        pieces = []
        for part in range(2):
            halves = [
                pltpu.roll(
                    lines[part], chunk * CHUNK + look + LOOK * half + 1, 1, stride=2 * LOOK, stride_axis=0
                )
                for half in range(2)
            ]
            pieces.append(jnp.concatenate(halves, axis=0))
        real, imag = pieces
        band_ref[0, m : m + 16, :] = real.astype(jnp.bfloat16)
        band_ref[0, BLOCK + m : BLOCK + m + 16, :] = imag.astype(jnp.bfloat16)
        band_ref[1, m : m + 16, :] = (-imag).astype(jnp.bfloat16)
        band_ref[1, BLOCK + m : BLOCK + m + 16, :] = real.astype(jnp.bfloat16)


def filter_block(band, first, second):
    both = jnp.dot(band[0], first, preferred_element_type=jnp.float32)
    both += jnp.dot(band[1], second, preferred_element_type=jnp.float32)
    return both.astype(jnp.bfloat16)


def interior_kernel(taps_ref, image_ref, out_ref, band_out_ref, ordered):
    a = pl.program_id(0)
    rows = image_ref.shape[2]
    order = column_order(image_ref.shape[3])
    for acq in range(taps_ref.shape[1]):

        @pl.when(a == acq)
        def _():
            fill_bands(taps_ref, band_out_ref.at[0], acq)

    for part in range(2):
        ordered[part] = jnp.dot(
            image_ref[part, 0], order, preferred_element_type=jnp.float32
        ).astype(jnp.bfloat16)
    band = band_out_ref[0]
    for block in range(1, rows // BLOCK - 1):
        window = pl.ds(block * BLOCK - HALO, 2 * BLOCK)
        both = filter_block(band, ordered[0, window, :], ordered[1, window, :])
        for chunk in range(2):
            for part in range(2):
                start = part * BLOCK + chunk * CHUNK
                out_ref[2 * block + chunk, part, 0] = both[start : start + CHUNK]


def edge_kernel(band_ref, inner_ref, halo_ref, filled_ref, out_ref):
    del filled_ref
    e = pl.program_id(0)
    order = column_order(inner_ref.shape[4])
    for acq in range(inner_ref.shape[2]):
        band = band_ref[acq]

        def put(windows):
            parts = [
                jnp.dot(w, order, preferred_element_type=jnp.float32).astype(jnp.bfloat16) for w in windows
            ]
            both = filter_block(band, parts[0], parts[1])
            for chunk in range(2):
                for part in range(2):
                    start = part * BLOCK + chunk * CHUNK
                    out_ref[chunk, part, acq] = both[start : start + CHUNK]

        @pl.when(e == 0)
        def _():
            put([jnp.concatenate([halo_ref[0, p, acq], inner_ref[0, p, acq]], axis=0) for p in range(2)])

        @pl.when(e == 1)
        def _():
            put([jnp.concatenate([inner_ref[0, p, acq], halo_ref[0, p, acq]], axis=0) for p in range(2)])


def pair_kernel(second_ref, map_ref, got_ref, out_ref, image, phase):
    groups, _, slots = got_ref.shape[:3]

    def widen(g, carry):
        for slot in range(slots):
            for part in range(2):
                image[part, g * slots + slot] = got_ref[g, part, slot].astype(jnp.float32)
        return carry

    lax.fori_loop(0, groups, widen, 0)
    lane = lax.broadcasted_iota(jnp.int32, (8, 128), 1)
    low = lane < 64

    def fold(value):
        upper, lower = value[:8], value[8:]
        return jnp.where(low, upper, lower) + pltpu.roll(jnp.where(low, lower, upper), 64, 1)

    def one_reference(i, carry):
        others = [second_ref[i * REACH + j] for j in range(REACH)]
        real = [None] * REACH
        imag = [None] * REACH
        for look in range(LOOK):
            for side in range(2):
                where = (pl.ds(look * 16, 16), pl.ds(side * 128, 128))
                a_re, a_im = (image[part, i, where[0], where[1]] for part in range(2))
                for j, k in enumerate(others):
                    b_re, b_im = (image[part, k, where[0], where[1]] for part in range(2))
                    re = a_re * b_re + a_im * b_im
                    im = a_im * b_re - a_re * b_im
                    real[j] = re if real[j] is None else real[j] + re
                    imag[j] = im if imag[j] is None else imag[j] + im
        for j in range(REACH):
            re, im = fold(real[j]), fold(imag[j])
            least = float(LOOK**4)
            ratio = im * lax.rsqrt(jnp.maximum(re * re + im * im, least))
            phase[pl.ds(pl.multiple_of((i * REACH + j) * 8, 8), 8), :] = ratio
        return carry

    lax.fori_loop(0, groups * slots, one_reference, 0)

    table = map_ref[...]
    acqs, pairs = table.shape
    high = table.astype(jnp.bfloat16)
    rest = (table - high.astype(jnp.float32)).astype(jnp.bfloat16)
    stacked = jnp.concatenate([high, rest], axis=0)
    for t in range(8):
        value = phase[pl.ds(t, pairs, stride=8), :]
        v_high = value.astype(jnp.bfloat16)
        v_rest = (value - v_high.astype(jnp.float32)).astype(jnp.bfloat16)
        both = jnp.dot(stacked, v_high, preferred_element_type=jnp.float32)
        total = both[:acqs] + both[acqs:] + jnp.dot(high, v_rest, preferred_element_type=jnp.float32)
        out_ref[:, t * 128 : (t + 1) * 128] = total


def inverse_of(pair_list, total_acq):
    labels = jnp.arange(total_acq, dtype=jnp.int32)
    incidence = (pair_list[:, 1:2] == labels).astype(jnp.float32) - (pair_list[:, 0:1] == labels).astype(jnp.float32)
    normal = jnp.dot(
        incidence.T, incidence, precision=lax.Precision.HIGHEST, preferred_element_type=jnp.float32
    ) + RIDGE * jnp.eye(total_acq, dtype=jnp.float32)
    lower = jnp.linalg.cholesky(normal)
    partial_solve = lax.linalg.triangular_solve(lower, incidence.T, left_side=True, lower=True)
    return lax.linalg.triangular_solve(lower, partial_solve, left_side=True, lower=True, transpose_a=True)


def per_device(radar_stack, band_taps, pair_list):
    groups = lax.axis_size("acq")
    blocks_az = lax.axis_size("az")
    _, local, rows, columns = radar_stack.shape
    up = [(i, i + 1) for i in range(blocks_az - 1)]
    down = [(j, i) for i, j in up]
    before = lax.ppermute(radar_stack[:, :, rows - HALO :], "az", up)
    after = lax.ppermute(radar_stack[:, :, :HALO], "az", down)
    taps = jnp.pad(band_taps.astype(jnp.float32), ((0, 0), (0, 0), (0, 2 * BLOCK - band_taps.shape[2])))

    filtered, band = pl.pallas_call(
        interior_kernel,
        grid=(local,),
        in_specs=[
            pl.BlockSpec((2, local, 2 * BLOCK), lambda a: (0, 0, 0)),
            pl.BlockSpec((2, 1, rows, columns), lambda a: (0, a, 0, 0)),
        ],
        out_specs=[
            pl.BlockSpec((groups, 2, 1, CHUNK, columns), lambda a: (0, 0, a, 0, 0)),
            pl.BlockSpec((1, 2, 2 * BLOCK, 2 * BLOCK), lambda a: (a, 0, 0, 0)),
        ],
        out_shape=[
            jax.ShapeDtypeStruct((groups, 2, local, CHUNK, columns), jnp.bfloat16),
            jax.ShapeDtypeStruct((local, 2, 2 * BLOCK, 2 * BLOCK), jnp.bfloat16),
        ],
        scratch_shapes=[pltpu.VMEM((2, rows, columns), jnp.bfloat16)],
        compiler_params=pltpu.CompilerParams(vmem_limit_bytes=40 * MIB),
        cost_estimate=pl.CostEstimate(flops=3_000_000_000, bytes_accessed=9_000_000, transcendentals=0),
        name="filter_interior",
    )(taps, radar_stack)

    near = 2 * BLOCK - HALO
    inner = jnp.stack([radar_stack[:, :, :near], radar_stack[:, :, rows - near :]])
    halo = jnp.stack([before, after])
    last = groups // 2 - 1
    filtered = pl.pallas_call(
        edge_kernel,
        grid=(2,),
        in_specs=[
            pl.BlockSpec((local, 2, 2 * BLOCK, 2 * BLOCK), lambda e: (0, 0, 0, 0)),
            pl.BlockSpec((1, 2, local, near, columns), lambda e: (e, 0, 0, 0, 0)),
            pl.BlockSpec((1, 2, local, HALO, columns), lambda e: (e, 0, 0, 0, 0)),
            pl.BlockSpec(memory_space=pl.ANY),
        ],
        out_specs=pl.BlockSpec((2, 2, local, CHUNK, columns), lambda e: (e * last, 0, 0, 0, 0)),
        out_shape=jax.ShapeDtypeStruct(filtered.shape, filtered.dtype),
        input_output_aliases={3: 0},
        compiler_params=pltpu.CompilerParams(vmem_limit_bytes=40 * MIB),
        cost_estimate=pl.CostEstimate(flops=900_000_000, bytes_accessed=5_000_000, transcendentals=0),
        name="filter_edges",
    )(band, inner, halo, filtered)

    got = lax.all_to_all(filtered, "acq", 0, 0, tiled=True)
    inverse_map = inverse_of(pair_list, groups * local)

    return pl.pallas_call(
        pair_kernel,
        in_specs=[
            pl.BlockSpec(memory_space=pltpu.SMEM),
            pl.BlockSpec(memory_space=pltpu.VMEM),
            pl.BlockSpec(memory_space=pltpu.VMEM),
        ],
        out_specs=pl.BlockSpec(memory_space=pltpu.VMEM),
        out_shape=jax.ShapeDtypeStruct((groups * local, CHUNK // LOOK * columns // LOOK), jnp.float32),
        scratch_shapes=[
            pltpu.VMEM((2, groups * local, CHUNK, columns), jnp.float32),
            pltpu.VMEM((pair_list.shape[0] * 8, 128), jnp.float32),
        ],
        compiler_params=pltpu.CompilerParams(vmem_limit_bytes=40 * MIB),
        cost_estimate=pl.CostEstimate(flops=100_000_000, bytes_accessed=5_000_000, transcendentals=300_000),
        name="pairs_and_inversion",
    )(pair_list[:, 1], inverse_map, got)


def solution(mesh):
    return jax.shard_map(
        per_device,
        mesh=mesh,
        in_specs=(P(None, "acq", "az", None), P(None, "acq", None), P()),
        out_specs=P(None, ("az", "acq")),
        check_vma=False,
    )
```

```python
import jax
import jax.numpy as jnp
from jax import lax
from jax.experimental import pallas as pl
from jax.experimental.pallas import tpu as pltpu
from jax.sharding import PartitionSpec as P

LOOK = 4
REACH = 4
BLOCK = 128
CHUNK = 64
HALO = 64
REST = 2 * BLOCK - HALO
CORES = 2
SOLVER_STEPS = 3
RIDGE = 1.0
MIB = 1 << 20
VMEM = pl.BlockSpec(memory_space=pltpu.VMEM)
SMEM = pl.BlockSpec(memory_space=pltpu.SMEM)
HBM = pl.BlockSpec(memory_space=pltpu.HBM)


def column_order(columns):
    source = lax.broadcasted_iota(jnp.int32, (columns, columns), 0)
    target = lax.broadcasted_iota(jnp.int32, (columns, columns), 1)
    looked = columns // LOOK
    wanted = (target % looked) * LOOK + target // looked
    return jnp.where(source == wanted, 1.0, 0.0).astype(jnp.bfloat16)


def fill_bands(taps_ref, band_ref, a):
    lines = [jnp.broadcast_to(taps_ref[part, a : a + 1, :], (8, 2 * BLOCK)) for part in range(2)]
    for m in range(0, BLOCK, 16):
        chunk, look = m // CHUNK, m % CHUNK // 16
        pieces = []
        for part in range(2):
            halves = [
                pltpu.roll(
                    lines[part], chunk * CHUNK + look + LOOK * half + 1, 1, stride=2 * LOOK, stride_axis=0
                )
                for half in range(2)
            ]
            pieces.append(jnp.concatenate(halves, axis=0))
        real, imag = pieces
        band_ref[0, m : m + 16, :] = real.astype(jnp.bfloat16)
        band_ref[0, BLOCK + m : BLOCK + m + 16, :] = imag.astype(jnp.bfloat16)
        band_ref[1, m : m + 16, :] = (-imag).astype(jnp.bfloat16)
        band_ref[1, BLOCK + m : BLOCK + m + 16, :] = real.astype(jnp.bfloat16)


def place_of(group_ref):
    group = group_ref[0]
    return group // (CHIPS * CORES), group // CORES % CHIPS, group % CORES


def elimination(pairs_ref, map_ref):
    total = map_ref.shape[0]
    label = lax.broadcasted_iota(jnp.int32, map_ref.shape, 0)
    incidence = jnp.where(label == pairs_ref[1:2, :], 1.0, 0.0) - jnp.where(label == pairs_ref[0:1, :], 1.0, 0.0)
    exact = incidence.astype(jnp.bfloat16)
    normal = lax.dot_general(exact, exact, (((1,), (1,)), ((), ())), preferred_element_type=jnp.float32)
    row = lax.broadcasted_iota(jnp.int32, (total, total), 0)
    column = lax.broadcasted_iota(jnp.int32, (total, total), 1)
    unit = jnp.where(row == column, 1.0, 0.0)
    table = jnp.concatenate([normal + RIDGE * unit, unit], axis=1)
    index = lax.broadcasted_iota(jnp.int32, table.shape, 0)
    for k in range(total):
        scaled = table[k : k + 1, :] * (1.0 / table[k : k + 1, k : k + 1])
        table = jnp.where(index == k, scaled, table - table[:, k : k + 1] * scaled)
        yield
    map_ref[...] = jnp.dot(
        table[:, total:], incidence, precision=lax.Precision.HIGHEST, preferred_element_type=jnp.float32
    )


def filter_window(band_ref, a, windows):
    both = jnp.dot(band_ref[a, 0], windows[0], preferred_element_type=jnp.float32)
    both += jnp.dot(band_ref[a, 1], windows[1], preferred_element_type=jnp.float32)
    return both.astype(jnp.bfloat16)


def interior_kernel(
    taps_ref, pairs_ref, image_ref, out_ref, band_ref, edge_ref, map_ref, image, ordered, done, arrived, left
):
    _, local, rows, columns = image.shape
    blocks = rows // BLOCK
    inward = [pltpu.make_async_copy(image_ref.at[:, a], image.at[:, a], arrived.at[a]) for a in range(local)]
    inner = pl.ds(CORES, CORES * (blocks - 2))
    outward = [pltpu.make_async_copy(done.at[a], out_ref.at[inner, :, a], left.at[a]) for a in range(local)]
    for copy in inward:
        copy.start()
    order = column_order(columns)
    solver = elimination(pairs_ref, map_ref)
    for a in range(local):
        fill_bands(taps_ref, band_ref.at[a], a)
        inward[a].wait()
        for part in range(2):
            ordered[part] = jnp.dot(image[part, a], order, preferred_element_type=jnp.float32).astype(jnp.bfloat16)
            edge_ref[0, part, a] = ordered[part, :REST, :]
            edge_ref[1, part, a] = ordered[part, rows - REST :, :]
        for block in range(1, blocks - 1):
            window = pl.ds(block * BLOCK - HALO, 2 * BLOCK)
            both = filter_window(band_ref, a, [ordered[part, window, :] for part in range(2)])
            for core in range(CORES):
                for part in range(2):
                    start = part * BLOCK + core * CHUNK
                    done[a, (block - 1) * CORES + core, part] = both[start : start + CHUNK]
            for _ in range(SOLVER_STEPS):
                next(solver, None)
        outward[a].start()
    for _ in solver:
        pass
    for copy in outward:
        copy.wait()


def edge_kernel(band_ref, edge_ref, before_ref, after_ref, filled_ref, out_ref, done, left):
    del filled_ref
    local, columns = before_ref.shape[1], before_ref.shape[3]
    order = column_order(columns)
    copies = []
    for e, halo_ref in enumerate((before_ref, after_ref)):
        halo = []
        for part in range(2):
            flat = halo_ref[part].reshape(local * HALO, columns)
            halo.append(jnp.dot(flat, order, preferred_element_type=jnp.float32).astype(jnp.bfloat16))
        for a in range(local):
            windows = []
            for part in range(2):
                pieces = [halo[part][a * HALO : (a + 1) * HALO], edge_ref[e, part, a]]
                windows.append(jnp.concatenate(pieces if e == 0 else pieces[::-1], axis=0))
            both = filter_window(band_ref, a, windows)
            for core in range(CORES):
                for part in range(2):
                    start = part * BLOCK + core * CHUNK
                    done[e, core, part, a] = both[start : start + CHUNK]
        share = pl.ds(e * (out_ref.shape[0] - CORES), CORES)
        copies.append(pltpu.make_async_copy(done.at[e], out_ref.at[share], left.at[e]))
        copies[-1].start()
    for copy in copies:
        copy.wait()


def pair_kernel(pairs_ref, map_ref, got_ref, out_ref, got, image, phase, arrived):
    groups, _, slots = got.shape[:3]
    copies = [pltpu.make_async_copy(got_ref.at[g], got.at[g], arrived.at[g]) for g in range(groups)]
    for copy in copies:
        copy.start()
    for g in range(groups):
        copies[g].wait()
        for slot in range(slots):
            k = g * slots + slot
            real = got[g, 0, slot].astype(jnp.float32)
            imag = got[g, 1, slot].astype(jnp.float32)
            image[0, k] = real
            image[1, k] = imag
            image[2, k] = real + imag
            image[3, k] = real - imag
    lane = lax.broadcasted_iota(jnp.int32, (8, 128), 1)
    low = lane < 64

    def fold(value):
        upper, lower = value[:8], value[8:]
        return jnp.where(low, upper, lower) + pltpu.roll(jnp.where(low, lower, upper), 64, 1)

    def plus(total, term):
        return term if total is None else total + term

    def one_reference(i, carry):
        others = [pairs_ref[1, i * REACH + j] for j in range(REACH)]
        shared, first, second = [None] * REACH, [None] * REACH, [None] * REACH
        for look in range(LOOK):
            for side in range(2):
                where = (pl.ds(look * 16, 16), pl.ds(side * 128, 128))
                a_re, a_im, a_sum = (image[plane, i, where[0], where[1]] for plane in range(3))
                for j, k in enumerate(others):
                    b_re, b_sum, b_less = (image[plane, k, where[0], where[1]] for plane in (0, 2, 3))
                    shared[j] = plus(shared[j], b_re * a_sum)
                    first[j] = plus(first[j], a_im * b_less)
                    second[j] = plus(second[j], a_re * b_sum)
        for j in range(REACH):
            re, im = fold(shared[j] - first[j]), fold(shared[j] - second[j])
            least = float(LOOK**4)
            ratio = im * lax.rsqrt(jnp.maximum(re * re + im * im, least))
            phase[pl.ds(pl.multiple_of((i * REACH + j) * 8, 8), 8), :] = ratio
        return carry

    lax.fori_loop(0, groups * slots, one_reference, 0, unroll=8)

    table = map_ref[...]
    acqs, pairs = table.shape
    high = table.astype(jnp.bfloat16)
    rest = (table - high.astype(jnp.float32)).astype(jnp.bfloat16)
    stacked = jnp.concatenate([high, rest], axis=0)
    for t in range(8):
        value = phase[pl.ds(t, pairs, stride=8), :]
        v_high = value.astype(jnp.bfloat16)
        v_rest = (value - v_high.astype(jnp.float32)).astype(jnp.bfloat16)
        both = jnp.dot(stacked, v_high, preferred_element_type=jnp.float32)
        total = both[:acqs] + both[acqs:] + jnp.dot(high, v_rest, preferred_element_type=jnp.float32)
        out_ref[:, t * 128 : (t + 1) * 128] = total


def per_device(radar_stack, band_taps, pair_list):
    blocks_az = lax.axis_size("az")
    groups = lax.axis_size("acq")
    _, local, rows, columns = radar_stack.shape
    total_acq = groups * local
    up = [(i, i + 1) for i in range(blocks_az - 1)]
    down = [(j, i) for i, j in up]
    before = lax.ppermute(radar_stack[:, :, rows - HALO :], "az", up)
    after = lax.ppermute(radar_stack[:, :, :HALO], "az", down)
    taps = jnp.pad(band_taps.astype(jnp.float32), ((0, 0), (0, 0), (0, 2 * BLOCK - band_taps.shape[2])))
    pairs = pair_list.T
    bf16, f32 = jnp.bfloat16, jnp.float32

    def settings(mib):
        return dict(
            compiler_params=pltpu.CompilerParams(vmem_limit_bytes=mib * MIB),
            cost_estimate=pl.CostEstimate(flops=2_000_000_000, bytes_accessed=9_000_000, transcendentals=0),
        )

    def in_hbm(value):
        return pltpu.with_memory_space_constraint(value, pltpu.HBM)

    inner = groups - 2 * CORES
    filtered, band, edge, inverse_map = pl.pallas_call(
        interior_kernel,
        in_specs=[VMEM, VMEM, HBM],
        out_specs=[HBM, VMEM, VMEM, VMEM],
        out_shape=[
            pltpu.HBM((groups, 2, local, CHUNK, columns), bf16),
            pltpu.VMEM((local, 2, 2 * BLOCK, 2 * BLOCK), bf16),
            pltpu.VMEM((2, 2, local, REST, columns), bf16),
            jax.ShapeDtypeStruct((total_acq, pair_list.shape[0]), f32),
        ],
        scratch_shapes=[
            pltpu.VMEM(radar_stack.shape, bf16),
            pltpu.VMEM((2, rows, columns), bf16),
            pltpu.VMEM((local, inner, 2, CHUNK, columns), bf16),
            pltpu.SemaphoreType.DMA((local,)),
            pltpu.SemaphoreType.DMA((local,)),
        ],
        name="filter_interior",
        **settings(32),
    )(taps, pairs, in_hbm(radar_stack))
    filtered = pl.pallas_call(
        edge_kernel,
        in_specs=[VMEM] * 4 + [HBM],
        out_specs=HBM,
        out_shape=pltpu.HBM(filtered.shape, bf16),
        input_output_aliases={4: 0},
        scratch_shapes=[
            pltpu.VMEM((2, CORES, 2, local, CHUNK, columns), bf16),
            pltpu.SemaphoreType.DMA((2,)),
        ],
        name="filter_edges",
        **settings(24),
    )(band, edge, before, after, filtered)
    got = lax.all_to_all(filtered, "acq", 0, 0, tiled=True)
    return pl.pallas_call(
        pair_kernel,
        in_specs=[SMEM, VMEM, HBM],
        out_specs=VMEM,
        out_shape=jax.ShapeDtypeStruct((total_acq, CHUNK // LOOK * columns // LOOK), f32),
        scratch_shapes=[
            pltpu.VMEM((groups, 2, local, CHUNK, columns), bf16),
            pltpu.VMEM((4, total_acq, CHUNK, columns), f32),
            pltpu.VMEM((pair_list.shape[0] * 8, 128), f32),
            pltpu.SemaphoreType.DMA((groups,)),
        ],
        name="pairs_and_inversion",
        **settings(40),
    )(pairs, inverse_map, in_hbm(got))


def solution(mesh):
    return jax.shard_map(
        per_device,
        mesh=mesh,
        in_specs=(P(None, "acq", "az", None), P(None, "acq", None), P()),
        out_specs=P(None, ("az", "acq")),
        check_vma=False,
    )
```

```python
import jax
import jax.numpy as jnp
from jax import lax
from jax.experimental import pallas as pl
from jax.experimental.pallas import tpu as pltpu
from jax.sharding import PartitionSpec as P

LOOK = 4
REACH = 4
BLOCK = 128
CHUNK = 64
HALO = 64
REST = 2 * BLOCK - HALO
CORES = 2
SOLVER_STEPS = 2
RIDGE = 1.0
MIB = 1 << 20
VMEM = pl.BlockSpec(memory_space=pltpu.VMEM)
SMEM = pl.BlockSpec(memory_space=pltpu.SMEM)
HBM = pl.BlockSpec(memory_space=pltpu.HBM)


def column_order(columns):
    source = lax.broadcasted_iota(jnp.int32, (columns, columns), 0)
    target = lax.broadcasted_iota(jnp.int32, (columns, columns), 1)
    looked = columns // LOOK
    wanted = (target % looked) * LOOK + target // looked
    return jnp.where(source == wanted, 1.0, 0.0).astype(jnp.bfloat16)


def fill_bands(taps_ref, band_ref, a):
    lines = [jnp.broadcast_to(taps_ref[part, a : a + 1, :], (8, 2 * BLOCK)) for part in range(2)]
    for m in range(0, BLOCK, 16):
        chunk, look = m // CHUNK, m % CHUNK // 16
        pieces = []
        for part in range(2):
            halves = [
                pltpu.roll(
                    lines[part], chunk * CHUNK + look + LOOK * half + 1, 1, stride=2 * LOOK, stride_axis=0
                )
                for half in range(2)
            ]
            pieces.append(jnp.concatenate(halves, axis=0))
        real, imag = pieces
        band_ref[0, m : m + 16, :] = real.astype(jnp.bfloat16)
        band_ref[0, BLOCK + m : BLOCK + m + 16, :] = imag.astype(jnp.bfloat16)
        band_ref[1, m : m + 16, :] = (-imag).astype(jnp.bfloat16)
        band_ref[1, BLOCK + m : BLOCK + m + 16, :] = real.astype(jnp.bfloat16)


def place_of(group_ref):
    group = group_ref[0]
    return group // (CHIPS * CORES), group // CORES % CHIPS, group % CORES


def elimination(pairs, map_ref):
    total = map_ref.shape[0]
    label = lax.broadcasted_iota(jnp.int32, map_ref.shape, 0)
    incidence = jnp.where(label == pairs[1:2, :], 1.0, 0.0) - jnp.where(label == pairs[0:1, :], 1.0, 0.0)
    exact = incidence.astype(jnp.bfloat16)
    normal = lax.dot_general(exact, exact, (((1,), (1,)), ((), ())), preferred_element_type=jnp.float32)
    row = lax.broadcasted_iota(jnp.int32, (total, total), 0)
    column = lax.broadcasted_iota(jnp.int32, (total, total), 1)
    unit = jnp.where(row == column, 1.0, 0.0)
    table = jnp.concatenate([normal + RIDGE * unit, unit], axis=1)
    index = lax.broadcasted_iota(jnp.int32, table.shape, 0)
    for k in range(total):
        scaled = table[k : k + 1, :] * (1.0 / table[k : k + 1, k : k + 1])
        table = jnp.where(index == k, scaled, table - table[:, k : k + 1] * scaled)
        yield
    map_ref[...] = jnp.dot(
        table[:, total:], incidence, precision=lax.Precision.HIGHEST, preferred_element_type=jnp.float32
    )


def filter_window(band_ref, a, windows):
    both = jnp.dot(band_ref[a, 0], windows[0], preferred_element_type=jnp.float32)
    both += jnp.dot(band_ref[a, 1], windows[1], preferred_element_type=jnp.float32)
    return both.astype(jnp.bfloat16)


def interior_kernel(
    taps_ref, pairs_ref, image_ref, out_ref, band_ref, edge_ref, map_ref, pairs, image, ordered, done, arrived, left
):
    _, local, rows, columns = image.shape
    blocks = rows // BLOCK
    inward = [pltpu.make_async_copy(image_ref.at[:, a], image.at[:, a], arrived.at[a]) for a in range(local)]
    inner = pl.ds(CORES, CORES * (blocks - 2))
    outward = [pltpu.make_async_copy(done.at[a], out_ref.at[inner, :, a], left.at[a]) for a in range(local)]
    listed = pltpu.make_async_copy(pairs_ref, pairs, arrived.at[local])
    listed.start()
    for copy in inward:
        copy.start()
    order = column_order(columns)
    fill_bands(taps_ref, band_ref.at[0], 0)
    listed.wait()
    solver = elimination(pairs[...], map_ref)

    def solve(steps):
        for _ in range(steps):
            next(solver, None)

    for a in range(1, local):
        fill_bands(taps_ref, band_ref.at[a], a)
        solve(SOLVER_STEPS)
    for a in range(local):
        inward[a].wait()
        for part in range(2):
            ordered[part] = jnp.dot(image[part, a], order, preferred_element_type=jnp.float32).astype(jnp.bfloat16)
            solve(SOLVER_STEPS)
            edge_ref[0, part, a] = ordered[part, :REST, :]
            edge_ref[1, part, a] = ordered[part, rows - REST :, :]
        for block in range(1, blocks - 1):
            window = pl.ds(block * BLOCK - HALO, 2 * BLOCK)
            both = filter_window(band_ref, a, [ordered[part, window, :] for part in range(2)])
            for core in range(CORES):
                for part in range(2):
                    start = part * BLOCK + core * CHUNK
                    done[a, (block - 1) * CORES + core, part] = both[start : start + CHUNK]
            solve(SOLVER_STEPS)
        outward[a].start()
    solve(1 + 8 * REST)
    for copy in outward:
        copy.wait()


def edge_kernel(odd_ref, band_ref, edge_ref, even_ref, odd_pairs_ref, filled_ref, out_ref, done, left):
    del filled_ref
    local, columns = even_ref.shape[1], even_ref.shape[3]
    order = column_order(columns)
    copies = []
    received = []
    for halo_ref in (even_ref, odd_pairs_ref):
        flat = (halo_ref[part].reshape(local * HALO, columns) for part in range(2))
        received.append([jnp.dot(f, order, preferred_element_type=jnp.float32).astype(jnp.bfloat16) for f in flat])
    for e in range(2):
        halo = [jnp.where(odd_ref[0] == 1 - e, one, two) for one, two in zip(*received)]
        for a in range(local):
            windows = []
            for part in range(2):
                pieces = [halo[part][a * HALO : (a + 1) * HALO], edge_ref[e, part, a]]
                windows.append(jnp.concatenate(pieces if e == 0 else pieces[::-1], axis=0))
            both = filter_window(band_ref, a, windows)
            for core in range(CORES):
                for part in range(2):
                    start = part * BLOCK + core * CHUNK
                    done[e, core, part, a] = both[start : start + CHUNK]
        share = pl.ds(e * (out_ref.shape[0] - CORES), CORES)
        copies.append(pltpu.make_async_copy(done.at[e], out_ref.at[share], left.at[e]))
        copies[-1].start()
    for copy in copies:
        copy.wait()


def pair_kernel(pairs_ref, map_ref, got, out_ref, image, phase):
    groups, _, slots = got.shape[:3]

    def widen(g, slot):
        k = g * slots + slot
        real = got[g, 0, slot].astype(jnp.float32)
        imag = got[g, 1, slot].astype(jnp.float32)
        image[0, k] = real
        image[1, k] = imag
        image[2, k] = real - imag

    lane = lax.broadcasted_iota(jnp.int32, (8, 128), 1)
    low = lane < 64

    def fold(value):
        upper, lower = value[:8], value[8:]
        return jnp.where(low, upper, lower) + pltpu.roll(jnp.where(low, lower, upper), 64, 1)

    def plus(total, term):
        return term if total is None else total + term

    def one_reference(i):
        others = [pairs_ref[1, i * REACH + j] for j in range(REACH)]
        reals, imags, crossed = [None] * REACH, [None] * REACH, [None] * REACH
        for look in range(LOOK):
            for side in range(2):
                where = (pl.ds(look * 16, 16), pl.ds(side * 128, 128))
                a_re, a_im = (image[plane, i, where[0], where[1]] for plane in range(2))
                a_sum = a_re + a_im
                for j, k in enumerate(others):
                    b_re, b_im, b_less = (image[plane, k, where[0], where[1]] for plane in range(3))
                    reals[j] = plus(reals[j], a_re * b_re)
                    imags[j] = plus(imags[j], a_im * b_im)
                    crossed[j] = plus(crossed[j], a_sum * b_less)
        for j in range(REACH):
            re = fold(reals[j] + imags[j])
            im = fold(crossed[j] - reals[j] + imags[j])
            least = float(LOOK**4)
            ratio = im * lax.rsqrt(jnp.maximum(re * re + im * im, least))
            phase[pl.ds(pl.multiple_of((i * REACH + j) * 8, 8), 8), :] = ratio

    for g in range(groups):
        for slot in range(slots):
            widen(g, slot)
    lax.fori_loop(0, groups * slots, lambda i, carry: one_reference(i), None, unroll=8)

    table = map_ref[...]
    acqs, pairs = table.shape
    high = table.astype(jnp.bfloat16)
    rest = (table - high.astype(jnp.float32)).astype(jnp.bfloat16)
    stacked = jnp.concatenate([high, rest], axis=0)
    for t in range(8):
        value = phase[pl.ds(t, pairs, stride=8), :]
        v_high = value.astype(jnp.bfloat16)
        v_rest = (value - v_high.astype(jnp.float32)).astype(jnp.bfloat16)
        both = jnp.dot(stacked, v_high, preferred_element_type=jnp.float32)
        total = both[:acqs] + both[acqs:] + jnp.dot(high, v_rest, preferred_element_type=jnp.float32)
        out_ref[:, t * 128 : (t + 1) * 128] = total


def per_device(radar_stack, band_taps, pair_list):
    blocks_az = lax.axis_size("az")
    groups = lax.axis_size("acq")
    _, local, rows, columns = radar_stack.shape
    total_acq = groups * local
    odd = lax.axis_index("az") % 2
    first, final = radar_stack[:, :, :HALO], radar_stack[:, :, rows - HALO :]
    meet = [[(i, i + 1) for i in range(start, blocks_az - 1, 2)] for start in range(2)]
    even_pairs, odd_pairs = (
        lax.ppermute(jnp.where(odd == start, final, first), "az", ones + [(j, i) for i, j in ones])
        for start, ones in enumerate(meet)
    )
    taps = jnp.pad(band_taps.astype(jnp.float32), ((0, 0), (0, 0), (0, 2 * BLOCK - band_taps.shape[2])))
    pairs = pair_list.T
    bf16, f32 = jnp.bfloat16, jnp.float32

    def settings(mib):
        return dict(
            compiler_params=pltpu.CompilerParams(vmem_limit_bytes=mib * MIB),
            cost_estimate=pl.CostEstimate(flops=2_000_000_000, bytes_accessed=9_000_000, transcendentals=0),
        )

    def in_hbm(value):
        return pltpu.with_memory_space_constraint(value, pltpu.HBM)

    inner = groups - 2 * CORES
    filtered, band, edge, inverse_map = pl.pallas_call(
        interior_kernel,
        in_specs=[VMEM, HBM, HBM],
        out_specs=[HBM, VMEM, VMEM, VMEM],
        out_shape=[
            pltpu.HBM((groups, 2, local, CHUNK, columns), bf16),
            pltpu.VMEM((local, 2, 2 * BLOCK, 2 * BLOCK), bf16),
            pltpu.VMEM((2, 2, local, REST, columns), bf16),
            jax.ShapeDtypeStruct((total_acq, pair_list.shape[0]), f32),
        ],
        scratch_shapes=[
            pltpu.VMEM(pairs.shape, pairs.dtype),
            pltpu.VMEM(radar_stack.shape, bf16),
            pltpu.VMEM((2, rows, columns), bf16),
            pltpu.VMEM((local, inner, 2, CHUNK, columns), bf16),
            pltpu.SemaphoreType.DMA((local + 1,)),
            pltpu.SemaphoreType.DMA((local,)),
        ],
        name="filter_interior",
        **settings(32),
    )(taps, in_hbm(pairs), in_hbm(radar_stack))
    filtered = pl.pallas_call(
        edge_kernel,
        in_specs=[SMEM] + [VMEM] * 4 + [HBM],
        out_specs=HBM,
        out_shape=pltpu.HBM(filtered.shape, bf16),
        input_output_aliases={5: 0},
        scratch_shapes=[
            pltpu.VMEM((2, CORES, 2, local, CHUNK, columns), bf16),
            pltpu.SemaphoreType.DMA((2,)),
        ],
        name="filter_edges",
        **settings(24),
    )(odd.reshape(1), band, edge, even_pairs, odd_pairs, filtered)
    got = lax.all_to_all(filtered, "acq", 0, 0, tiled=True)
    return pl.pallas_call(
        pair_kernel,
        in_specs=[SMEM, VMEM, VMEM],
        out_specs=VMEM,
        out_shape=jax.ShapeDtypeStruct((total_acq, CHUNK // LOOK * columns // LOOK), f32),
        scratch_shapes=[
            pltpu.VMEM((3, total_acq, CHUNK, columns), f32),
            pltpu.VMEM((pair_list.shape[0] * 8, 128), f32),
        ],
        name="pairs_and_inversion",
        **settings(24),
    )(pairs, inverse_map, pltpu.with_memory_space_constraint(got, pltpu.VMEM))


def solution(mesh):
    return jax.shard_map(
        per_device,
        mesh=mesh,
        in_specs=(P(None, "acq", "az", None), P(None, "acq", None), P()),
        out_specs=P(None, ("az", "acq")),
        check_vma=False,
    )
```

```python
import jax
import jax.numpy as jnp
from jax import lax
from jax.experimental import pallas as pl
from jax.experimental.pallas import tpu as pltpu
from jax.sharding import PartitionSpec as P

LOOK = 4
REACH = 4
BLOCK = 128
CHUNK = 64
HALO = 64
REST = 2 * BLOCK - HALO
CORES = 2
AHEAD = 2
SOLVER_STEPS = 2
RIDGE = 1.0
MIB = 1 << 20
VMEM = pl.BlockSpec(memory_space=pltpu.VMEM)
SMEM = pl.BlockSpec(memory_space=pltpu.SMEM)
HBM = pl.BlockSpec(memory_space=pltpu.HBM)


def column_order(columns):
    source = lax.broadcasted_iota(jnp.int32, (columns, columns), 0)
    target = lax.broadcasted_iota(jnp.int32, (columns, columns), 1)
    looked = columns // LOOK
    wanted = (target % looked) * LOOK + target // looked
    return jnp.where(source == wanted, 1.0, 0.0).astype(jnp.bfloat16)


def fill_bands(taps_ref, band_ref, a):
    lines = [jnp.broadcast_to(taps_ref[part, a : a + 1, :], (8, 2 * BLOCK)) for part in range(2)]
    for m in range(0, BLOCK, 16):
        chunk, look = m // CHUNK, m % CHUNK // 16
        pieces = []
        for part in range(2):
            halves = [
                pltpu.roll(
                    lines[part], chunk * CHUNK + look + LOOK * half + 1, 1, stride=2 * LOOK, stride_axis=0
                )
                for half in range(2)
            ]
            pieces.append(jnp.concatenate(halves, axis=0))
        real, imag = pieces
        band_ref[0, m : m + 16, :] = real.astype(jnp.bfloat16)
        band_ref[0, BLOCK + m : BLOCK + m + 16, :] = imag.astype(jnp.bfloat16)
        band_ref[1, m : m + 16, :] = (-imag).astype(jnp.bfloat16)
        band_ref[1, BLOCK + m : BLOCK + m + 16, :] = real.astype(jnp.bfloat16)


def place_of(group_ref):
    group = group_ref[0]
    return group // (CHIPS * CORES), group // CORES % CHIPS, group % CORES


def elimination(pairs, map_ref):
    total = map_ref.shape[0]
    label = lax.broadcasted_iota(jnp.int32, map_ref.shape, 0)
    incidence = jnp.where(label == pairs[1:2, :], 1.0, 0.0) - jnp.where(label == pairs[0:1, :], 1.0, 0.0)
    exact = incidence.astype(jnp.bfloat16)
    normal = lax.dot_general(exact, exact, (((1,), (1,)), ((), ())), preferred_element_type=jnp.float32)
    row = lax.broadcasted_iota(jnp.int32, (total, total), 0)
    column = lax.broadcasted_iota(jnp.int32, (total, total), 1)
    unit = jnp.where(row == column, 1.0, 0.0)
    table = jnp.concatenate([normal + RIDGE * unit, unit], axis=1)
    index = lax.broadcasted_iota(jnp.int32, table.shape, 0)
    def spread(k):
        return jnp.broadcast_to(table[:, k : k + 1], table.shape)

    spreads = [spread(k) for k in range(AHEAD)]
    for k in range(total):
        if k + AHEAD < total:
            spreads.append(spread(k + AHEAD))
        pivot = spreads.pop(0)
        scale = 1.0 / pivot[k : k + 1, :]

        def step(value):
            scaled = value[k : k + 1, :] * scale
            return jnp.where(index == k, scaled, value - pivot * scaled)

        table = step(table)
        spreads = [step(value) for value in spreads]
        yield
    map_ref[...] = jnp.dot(
        table[:, total:], incidence, precision=lax.Precision.HIGHEST, preferred_element_type=jnp.float32
    )


def filter_window(band_ref, a, windows):
    both = jnp.dot(band_ref[a, 0], windows[0], preferred_element_type=jnp.float32)
    both += jnp.dot(band_ref[a, 1], windows[1], preferred_element_type=jnp.float32)
    return both.astype(jnp.bfloat16)


def interior_kernel(
    taps_ref, pairs_ref, image_ref, out_ref, band_ref, edge_ref, map_ref, pairs, image, ordered, done, arrived, left
):
    _, local, rows, columns = image.shape
    blocks = rows // BLOCK
    inward = [pltpu.make_async_copy(image_ref.at[:, a], image.at[:, a], arrived.at[a]) for a in range(local)]
    inner = pl.ds(CORES, CORES * (blocks - 2))
    outward = [pltpu.make_async_copy(done.at[a], out_ref.at[inner, :, a], left.at[a]) for a in range(local)]
    listed = pltpu.make_async_copy(pairs_ref, pairs, arrived.at[local])
    listed.start()
    for copy in inward:
        copy.start()
    order = column_order(columns)
    fill_bands(taps_ref, band_ref.at[0], 0)
    listed.wait()
    solver = elimination(pairs[...], map_ref)

    def solve(steps):
        for _ in range(steps):
            next(solver, None)

    for a in range(1, local):
        fill_bands(taps_ref, band_ref.at[a], a)
        solve(SOLVER_STEPS)
    for a in range(local):
        inward[a].wait()
        for part in range(2):
            ordered[part] = jnp.dot(image[part, a], order, preferred_element_type=jnp.float32).astype(jnp.bfloat16)
            solve(SOLVER_STEPS)
            edge_ref[0, part, a] = ordered[part, :REST, :]
            edge_ref[1, part, a] = ordered[part, rows - REST :, :]
        for block in range(1, blocks - 1):
            window = pl.ds(block * BLOCK - HALO, 2 * BLOCK)
            both = filter_window(band_ref, a, [ordered[part, window, :] for part in range(2)])
            for core in range(CORES):
                for part in range(2):
                    start = part * BLOCK + core * CHUNK
                    done[a, (block - 1) * CORES + core, part] = both[start : start + CHUNK]
            solve(SOLVER_STEPS)
        outward[a].start()
    solve(1 + 8 * REST)
    for copy in outward:
        copy.wait()


def edge_kernel(odd_ref, band_ref, edge_ref, even_ref, odd_pairs_ref, filled_ref, out_ref, done, left):
    del filled_ref
    local, columns = even_ref.shape[1], even_ref.shape[3]
    order = column_order(columns)
    copies = []
    received = []
    for halo_ref in (even_ref, odd_pairs_ref):
        flat = (halo_ref[part].reshape(local * HALO, columns) for part in range(2))
        received.append([jnp.dot(f, order, preferred_element_type=jnp.float32).astype(jnp.bfloat16) for f in flat])
    for e in range(2):
        halo = [jnp.where(odd_ref[0] == 1 - e, one, two) for one, two in zip(*received)]
        for a in range(local):
            windows = []
            for part in range(2):
                pieces = [halo[part][a * HALO : (a + 1) * HALO], edge_ref[e, part, a]]
                windows.append(jnp.concatenate(pieces if e == 0 else pieces[::-1], axis=0))
            both = filter_window(band_ref, a, windows)
            for core in range(CORES):
                for part in range(2):
                    start = part * BLOCK + core * CHUNK
                    done[e, core, part, a] = both[start : start + CHUNK]
        share = pl.ds(e * (out_ref.shape[0] - CORES), CORES)
        copies.append(pltpu.make_async_copy(done.at[e], out_ref.at[share], left.at[e]))
        copies[-1].start()
    for copy in copies:
        copy.wait()


def pair_kernel(pairs_ref, map_ref, got, out_ref, image, phase):
    groups, _, slots = got.shape[:3]

    def widen(g, slot):
        k = g * slots + slot
        real = got[g, 0, slot].astype(jnp.float32)
        imag = got[g, 1, slot].astype(jnp.float32)
        image[0, k] = real
        image[1, k] = imag
        image[2, k] = real - imag

    lane = lax.broadcasted_iota(jnp.int32, (8, 128), 1)
    low = lane < 64

    def fold(value):
        upper, lower = value[:8], value[8:]
        return jnp.where(low, upper, lower) + pltpu.roll(jnp.where(low, lower, upper), 64, 1)

    def plus(total, term):
        return term if total is None else total + term

    def one_reference(i):
        others = [pairs_ref[1, i * REACH + j] for j in range(REACH)]
        reals, imags, crossed = [None] * REACH, [None] * REACH, [None] * REACH
        for look in range(LOOK):
            for side in range(2):
                where = (pl.ds(look * 16, 16), pl.ds(side * 128, 128))
                a_re, a_im = (image[plane, i, where[0], where[1]] for plane in range(2))
                a_sum = a_re + a_im
                for j, k in enumerate(others):
                    b_re, b_im, b_less = (image[plane, k, where[0], where[1]] for plane in range(3))
                    reals[j] = plus(reals[j], a_re * b_re)
                    imags[j] = plus(imags[j], a_im * b_im)
                    crossed[j] = plus(crossed[j], a_sum * b_less)
        for j in range(REACH):
            re = fold(reals[j] + imags[j])
            im = fold(crossed[j] - reals[j] + imags[j])
            least = float(LOOK**4)
            ratio = im * lax.rsqrt(jnp.maximum(re * re + im * im, least))
            phase[pl.ds(pl.multiple_of((i * REACH + j) * 8, 8), 8), :] = ratio

    for g in range(groups):
        for slot in range(slots):
            widen(g, slot)
    lax.fori_loop(0, groups * slots, lambda i, carry: one_reference(i), None, unroll=8)

    table = map_ref[...]
    acqs, pairs = table.shape
    high = table.astype(jnp.bfloat16)
    rest = (table - high.astype(jnp.float32)).astype(jnp.bfloat16)
    stacked = jnp.concatenate([high, rest], axis=0)
    for t in range(8):
        value = phase[pl.ds(t, pairs, stride=8), :]
        v_high = value.astype(jnp.bfloat16)
        v_rest = (value - v_high.astype(jnp.float32)).astype(jnp.bfloat16)
        both = jnp.dot(stacked, v_high, preferred_element_type=jnp.float32)
        total = both[:acqs] + both[acqs:] + jnp.dot(high, v_rest, preferred_element_type=jnp.float32)
        out_ref[:, t * 128 : (t + 1) * 128] = total


def per_device(radar_stack, band_taps, pair_list):
    blocks_az = lax.axis_size("az")
    groups = lax.axis_size("acq")
    _, local, rows, columns = radar_stack.shape
    total_acq = groups * local
    odd = lax.axis_index("az") % 2
    meet = [[(i, i + 1) for i in range(start, blocks_az - 1, 2)] for start in range(2)]
    even_pairs, odd_pairs = (
        lax.ppermute(
            lax.dynamic_slice_in_dim(radar_stack, jnp.where(odd == start, rows - HALO, 0), HALO, 2),
            "az",
            ones + [(j, i) for i, j in ones],
        )
        for start, ones in enumerate(meet)
    )
    taps = jnp.pad(band_taps.astype(jnp.float32), ((0, 0), (0, 0), (0, 2 * BLOCK - band_taps.shape[2])))
    pairs = pair_list.T
    bf16, f32 = jnp.bfloat16, jnp.float32

    def settings(mib):
        return dict(
            compiler_params=pltpu.CompilerParams(vmem_limit_bytes=mib * MIB),
            cost_estimate=pl.CostEstimate(flops=2_000_000_000, bytes_accessed=9_000_000, transcendentals=0),
        )

    def in_hbm(value):
        return pltpu.with_memory_space_constraint(value, pltpu.HBM)

    inner = groups - 2 * CORES
    filtered, band, edge, inverse_map = pl.pallas_call(
        interior_kernel,
        in_specs=[VMEM, HBM, HBM],
        out_specs=[HBM, VMEM, VMEM, VMEM],
        out_shape=[
            pltpu.HBM((groups, 2, local, CHUNK, columns), bf16),
            pltpu.VMEM((local, 2, 2 * BLOCK, 2 * BLOCK), bf16),
            pltpu.VMEM((2, 2, local, REST, columns), bf16),
            jax.ShapeDtypeStruct((total_acq, pair_list.shape[0]), f32),
        ],
        scratch_shapes=[
            pltpu.VMEM(pairs.shape, pairs.dtype),
            pltpu.VMEM(radar_stack.shape, bf16),
            pltpu.VMEM((2, rows, columns), bf16),
            pltpu.VMEM((local, inner, 2, CHUNK, columns), bf16),
            pltpu.SemaphoreType.DMA((local + 1,)),
            pltpu.SemaphoreType.DMA((local,)),
        ],
        name="filter_interior",
        **settings(32),
    )(taps, in_hbm(pairs), in_hbm(radar_stack))
    filtered = pl.pallas_call(
        edge_kernel,
        in_specs=[SMEM] + [VMEM] * 4 + [HBM],
        out_specs=HBM,
        out_shape=pltpu.HBM(filtered.shape, bf16),
        input_output_aliases={5: 0},
        scratch_shapes=[
            pltpu.VMEM((2, CORES, 2, local, CHUNK, columns), bf16),
            pltpu.SemaphoreType.DMA((2,)),
        ],
        name="filter_edges",
        **settings(24),
    )(odd.reshape(1), band, edge, even_pairs, odd_pairs, filtered)
    got = lax.all_to_all(filtered, "acq", 0, 0, tiled=True)
    return pl.pallas_call(
        pair_kernel,
        in_specs=[SMEM, VMEM, VMEM],
        out_specs=VMEM,
        out_shape=jax.ShapeDtypeStruct((total_acq, CHUNK // LOOK * columns // LOOK), f32),
        scratch_shapes=[
            pltpu.VMEM((3, total_acq, CHUNK, columns), f32),
            pltpu.VMEM((pair_list.shape[0] * 8, 128), f32),
        ],
        name="pairs_and_inversion",
        **settings(24),
    )(pairs, inverse_map, pltpu.with_memory_space_constraint(got, pltpu.VMEM))


def solution(mesh):
    return jax.shard_map(
        per_device,
        mesh=mesh,
        in_specs=(P(None, "acq", "az", None), P(None, "acq", None), P()),
        out_specs=P(None, ("az", "acq")),
        check_vma=False,
    )
```

```python
import jax
import jax.numpy as jnp
from jax import lax
from jax.experimental import pallas as pl
from jax.experimental.pallas import tpu as pltpu
from jax.sharding import PartitionSpec as P

LOOK = 4
REACH = 4
BLOCK = 128
CHUNK = 64
HALO = 64
REST = 2 * BLOCK - HALO
CORES = 2
AHEAD = 2
SOLVER_STEPS = 2
RIDGE = 1.0
MIB = 1 << 20
VMEM = pl.BlockSpec(memory_space=pltpu.VMEM)
SMEM = pl.BlockSpec(memory_space=pltpu.SMEM)
HBM = pl.BlockSpec(memory_space=pltpu.HBM)


def column_order(columns):
    source = lax.broadcasted_iota(jnp.int32, (columns, columns), 0)
    target = lax.broadcasted_iota(jnp.int32, (columns, columns), 1)
    looked = columns // LOOK
    wanted = (target % looked) * LOOK + target // looked
    return jnp.where(source == wanted, 1.0, 0.0).astype(jnp.bfloat16)


def fill_bands(taps_ref, band_ref, a):
    lines = [jnp.broadcast_to(taps_ref[part, a : a + 1, :], (8, 2 * BLOCK)) for part in range(2)]
    for m in range(0, BLOCK, 16):
        chunk, look = m // CHUNK, m % CHUNK // 16
        pieces = []
        for part in range(2):
            halves = [
                pltpu.roll(
                    lines[part], chunk * CHUNK + look + LOOK * half + 1, 1, stride=2 * LOOK, stride_axis=0
                )
                for half in range(2)
            ]
            pieces.append(jnp.concatenate(halves, axis=0))
        real, imag = pieces
        band_ref[0, m : m + 16, :] = real.astype(jnp.bfloat16)
        band_ref[0, BLOCK + m : BLOCK + m + 16, :] = imag.astype(jnp.bfloat16)
        band_ref[1, m : m + 16, :] = (-imag).astype(jnp.bfloat16)
        band_ref[1, BLOCK + m : BLOCK + m + 16, :] = real.astype(jnp.bfloat16)


def place_of(group_ref):
    group = group_ref[0]
    return group // (CHIPS * CORES), group // CORES % CHIPS, group % CORES


def elimination(pairs, map_ref):
    total = map_ref.shape[0]
    label = lax.broadcasted_iota(jnp.int32, map_ref.shape, 0)
    incidence = jnp.where(label == pairs[1:2, :], 1.0, 0.0) - jnp.where(label == pairs[0:1, :], 1.0, 0.0)
    exact = incidence.astype(jnp.bfloat16)
    normal = lax.dot_general(exact, exact, (((1,), (1,)), ((), ())), preferred_element_type=jnp.float32)
    row = lax.broadcasted_iota(jnp.int32, (total, total), 0)
    column = lax.broadcasted_iota(jnp.int32, (total, total), 1)
    unit = jnp.where(row == column, 1.0, 0.0)
    table = jnp.concatenate([normal + RIDGE * unit, unit], axis=1)
    index = lax.broadcasted_iota(jnp.int32, table.shape, 0)
    def spread(k):
        return jnp.broadcast_to(table[:, k : k + 1], table.shape)

    spreads = [spread(k) for k in range(AHEAD)]
    for k in range(total):
        if k + AHEAD < total:
            spreads.append(spread(k + AHEAD))
        pivot = spreads.pop(0)
        scale = 1.0 / pivot[k : k + 1, :]

        def step(value):
            scaled = value[k : k + 1, :] * scale
            return jnp.where(index == k, scaled, value - pivot * scaled)

        table = step(table)
        spreads = [step(value) for value in spreads]
        yield
    map_ref[...] = jnp.dot(
        table[:, total:], incidence, precision=lax.Precision.HIGHEST, preferred_element_type=jnp.float32
    )


def filter_window(band_ref, a, windows):
    both = jnp.dot(band_ref[a, 0], windows[0], preferred_element_type=jnp.float32)
    both += jnp.dot(band_ref[a, 1], windows[1], preferred_element_type=jnp.float32)
    return both.astype(jnp.bfloat16)


def interior_kernel(
    taps_ref, pairs_ref, image_ref, out_ref, band_ref, edge_ref, map_ref, pairs, image, ordered, done, arrived, left
):
    _, local, rows, columns = image.shape
    blocks = rows // BLOCK
    inward = [pltpu.make_async_copy(image_ref.at[:, a], image.at[:, a], arrived.at[a]) for a in range(local)]
    inner = pl.ds(CORES, CORES * (blocks - 2))
    outward = [pltpu.make_async_copy(done.at[a], out_ref.at[inner, :, a], left.at[a]) for a in range(local)]
    listed = pltpu.make_async_copy(pairs_ref, pairs, arrived.at[local])
    listed.start()
    for copy in inward:
        copy.start()
    order = column_order(columns)
    fill_bands(taps_ref, band_ref.at[0], 0)
    listed.wait()
    solver = elimination(pairs[...], map_ref)

    def solve(steps):
        for _ in range(steps):
            next(solver, None)

    for a in range(1, local):
        fill_bands(taps_ref, band_ref.at[a], a)
        solve(SOLVER_STEPS)
    for a in range(local):
        inward[a].wait()
        for part in range(2):
            ordered[part] = jnp.dot(image[part, a], order, preferred_element_type=jnp.float32).astype(jnp.bfloat16)
            solve(SOLVER_STEPS)
            edge_ref[0, part, a] = ordered[part, :REST, :]
            edge_ref[1, part, a] = ordered[part, rows - REST :, :]
        for block in range(1, blocks - 1):
            window = pl.ds(block * BLOCK - HALO, 2 * BLOCK)
            both = filter_window(band_ref, a, [ordered[part, window, :] for part in range(2)])
            for core in range(CORES):
                for part in range(2):
                    start = part * BLOCK + core * CHUNK
                    done[a, (block - 1) * CORES + core, part] = both[start : start + CHUNK]
            solve(SOLVER_STEPS)
        outward[a].start()
    solve(1 + 8 * REST)
    for copy in outward:
        copy.wait()


def edge_kernel(odd_ref, band_ref, edge_ref, even_ref, odd_pairs_ref, filled_ref, out_ref, done, left):
    del filled_ref
    local, columns = even_ref.shape[1], even_ref.shape[3]
    order = column_order(columns)
    copies = []
    received = []
    for halo_ref in (even_ref, odd_pairs_ref):
        flat = (halo_ref[part].reshape(local * HALO, columns) for part in range(2))
        received.append([jnp.dot(f, order, preferred_element_type=jnp.float32).astype(jnp.bfloat16) for f in flat])
    for e in range(2):
        halo = [jnp.where(odd_ref[0] == 1 - e, one, two) for one, two in zip(*received)]
        for a in range(local):
            windows = []
            for part in range(2):
                pieces = [halo[part][a * HALO : (a + 1) * HALO], edge_ref[e, part, a]]
                windows.append(jnp.concatenate(pieces if e == 0 else pieces[::-1], axis=0))
            both = filter_window(band_ref, a, windows)
            for core in range(CORES):
                for part in range(2):
                    start = part * BLOCK + core * CHUNK
                    done[e, a, core, part] = both[start : start + CHUNK]
            share = pl.ds(e * (out_ref.shape[0] - CORES), CORES)
            copies.append(pltpu.make_async_copy(done.at[e, a], out_ref.at[share, :, a], left.at[e, a]))
            copies[-1].start()
    for copy in copies:
        copy.wait()


def pair_kernel(pairs_ref, map_ref, got, out_ref, image, phase):
    groups, _, slots = got.shape[:3]

    def widen(g, slot):
        k = g * slots + slot
        real = got[g, 0, slot].astype(jnp.float32)
        imag = got[g, 1, slot].astype(jnp.float32)
        image[0, k] = real
        image[1, k] = imag
        image[2, k] = real - imag

    lane = lax.broadcasted_iota(jnp.int32, (8, 128), 1)
    low = lane < 64

    def fold(value):
        upper, lower = value[:8], value[8:]
        return jnp.where(low, upper, lower) + pltpu.roll(jnp.where(low, lower, upper), 64, 1)

    def plus(total, term):
        return term if total is None else total + term

    def one_reference(i):
        others = [pairs_ref[1, i * REACH + j] for j in range(REACH)]
        reals, imags, crossed = [None] * REACH, [None] * REACH, [None] * REACH
        for look in range(LOOK):
            for side in range(2):
                where = (pl.ds(look * 16, 16), pl.ds(side * 128, 128))
                a_re, a_im = (image[plane, i, where[0], where[1]] for plane in range(2))
                a_sum = a_re + a_im
                for j, k in enumerate(others):
                    b_re, b_im, b_less = (image[plane, k, where[0], where[1]] for plane in range(3))
                    reals[j] = plus(reals[j], a_re * b_re)
                    imags[j] = plus(imags[j], a_im * b_im)
                    crossed[j] = plus(crossed[j], a_sum * b_less)
        for j in range(REACH):
            re = fold(reals[j] + imags[j])
            im = fold(crossed[j] - reals[j] + imags[j])
            least = float(LOOK**4)
            ratio = im * lax.rsqrt(jnp.maximum(re * re + im * im, least))
            phase[pl.ds(pl.multiple_of((i * REACH + j) * 8, 8), 8), :] = ratio

    for g in range(groups):
        for slot in range(slots):
            widen(g, slot)
    lax.fori_loop(0, groups * slots, lambda i, carry: one_reference(i), None, unroll=16)

    table = map_ref[...]
    acqs, pairs = table.shape
    high = table.astype(jnp.bfloat16)
    rest = (table - high.astype(jnp.float32)).astype(jnp.bfloat16)
    stacked = jnp.concatenate([high, rest], axis=0)
    for t in range(8):
        value = phase[pl.ds(t, pairs, stride=8), :]
        v_high = value.astype(jnp.bfloat16)
        v_rest = (value - v_high.astype(jnp.float32)).astype(jnp.bfloat16)
        both = jnp.dot(stacked, v_high, preferred_element_type=jnp.float32)
        total = both[:acqs] + both[acqs:] + jnp.dot(high, v_rest, preferred_element_type=jnp.float32)
        out_ref[:, t * 128 : (t + 1) * 128] = total


def per_device(radar_stack, band_taps, pair_list):
    blocks_az = lax.axis_size("az")
    groups = lax.axis_size("acq")
    _, local, rows, columns = radar_stack.shape
    total_acq = groups * local
    odd = lax.axis_index("az") % 2
    meet = [[(i, i + 1) for i in range(start, blocks_az - 1, 2)] for start in range(2)]
    even_pairs, odd_pairs = (
        lax.ppermute(
            lax.dynamic_slice_in_dim(radar_stack, jnp.where(odd == start, rows - HALO, 0), HALO, 2),
            "az",
            ones + [(j, i) for i, j in ones],
        )
        for start, ones in enumerate(meet)
    )
    taps = jnp.pad(band_taps.astype(jnp.float32), ((0, 0), (0, 0), (0, 2 * BLOCK - band_taps.shape[2])))
    pairs = pair_list.T
    bf16, f32 = jnp.bfloat16, jnp.float32

    def settings(mib):
        return dict(
            compiler_params=pltpu.CompilerParams(vmem_limit_bytes=mib * MIB),
            cost_estimate=pl.CostEstimate(flops=2_000_000_000, bytes_accessed=9_000_000, transcendentals=0),
        )

    def in_hbm(value):
        return pltpu.with_memory_space_constraint(value, pltpu.HBM)

    inner = groups - 2 * CORES
    filtered, band, edge, inverse_map = pl.pallas_call(
        interior_kernel,
        in_specs=[VMEM, HBM, HBM],
        out_specs=[HBM, VMEM, VMEM, VMEM],
        out_shape=[
            pltpu.HBM((groups, 2, local, CHUNK, columns), bf16),
            pltpu.VMEM((local, 2, 2 * BLOCK, 2 * BLOCK), bf16),
            pltpu.VMEM((2, 2, local, REST, columns), bf16),
            jax.ShapeDtypeStruct((total_acq, pair_list.shape[0]), f32),
        ],
        scratch_shapes=[
            pltpu.VMEM(pairs.shape, pairs.dtype),
            pltpu.VMEM(radar_stack.shape, bf16),
            pltpu.VMEM((2, rows, columns), bf16),
            pltpu.VMEM((local, inner, 2, CHUNK, columns), bf16),
            pltpu.SemaphoreType.DMA((local + 1,)),
            pltpu.SemaphoreType.DMA((local,)),
        ],
        name="filter_interior",
        **settings(32),
    )(taps, in_hbm(pairs), in_hbm(radar_stack))
    filtered = pl.pallas_call(
        edge_kernel,
        in_specs=[SMEM] + [VMEM] * 4 + [HBM],
        out_specs=HBM,
        out_shape=pltpu.HBM(filtered.shape, bf16),
        input_output_aliases={5: 0},
        scratch_shapes=[
            pltpu.VMEM((2, local, CORES, 2, CHUNK, columns), bf16),
            pltpu.SemaphoreType.DMA((2, local)),
        ],
        name="filter_edges",
        **settings(24),
    )(odd.reshape(1), band, edge, even_pairs, odd_pairs, filtered)
    got = lax.all_to_all(filtered, "acq", 0, 0, tiled=True)
    return pl.pallas_call(
        pair_kernel,
        in_specs=[SMEM, VMEM, VMEM],
        out_specs=VMEM,
        out_shape=jax.ShapeDtypeStruct((total_acq, CHUNK // LOOK * columns // LOOK), f32),
        scratch_shapes=[
            pltpu.VMEM((3, total_acq, CHUNK, columns), f32),
            pltpu.VMEM((pair_list.shape[0] * 8, 128), f32),
        ],
        name="pairs_and_inversion",
        **settings(24),
    )(pairs, inverse_map, pltpu.with_memory_space_constraint(got, pltpu.VMEM))


def solution(mesh):
    return jax.shard_map(
        per_device,
        mesh=mesh,
        in_specs=(P(None, "acq", "az", None), P(None, "acq", None), P()),
        out_specs=P(None, ("az", "acq")),
        check_vma=False,
    )
```

```python
import jax
import jax.numpy as jnp
from jax import lax
from jax.experimental import pallas as pl
from jax.experimental.pallas import tpu as pltpu
from jax.sharding import PartitionSpec as P

LOOK = 4
REACH = 4
BLOCK = 128
CHUNK = 64
HALO = 64
REST = 2 * BLOCK - HALO
CORES = 2
AHEAD = 2
SOLVER_STEPS = 2
RIDGE = 1.0
MIB = 1 << 20
VMEM = pl.BlockSpec(memory_space=pltpu.VMEM)
SMEM = pl.BlockSpec(memory_space=pltpu.SMEM)
HBM = pl.BlockSpec(memory_space=pltpu.HBM)


def column_order(columns):
    source = lax.broadcasted_iota(jnp.int32, (columns, columns), 0)
    target = lax.broadcasted_iota(jnp.int32, (columns, columns), 1)
    looked = columns // LOOK
    wanted = (target % looked) * LOOK + target // looked
    return jnp.where(source == wanted, 1.0, 0.0).astype(jnp.bfloat16)


def fill_bands(taps_ref, band_ref, a):
    lines = [jnp.broadcast_to(taps_ref[part, a : a + 1, :], (8, 2 * BLOCK)) for part in range(2)]
    for m in range(0, BLOCK, 16):
        chunk, look = m // CHUNK, m % CHUNK // 16
        pieces = []
        for part in range(2):
            halves = [
                pltpu.roll(
                    lines[part], chunk * CHUNK + look + LOOK * half + 1, 1, stride=2 * LOOK, stride_axis=0
                )
                for half in range(2)
            ]
            pieces.append(jnp.concatenate(halves, axis=0))
        real, imag = pieces
        band_ref[0, m : m + 16, :] = real.astype(jnp.bfloat16)
        band_ref[0, BLOCK + m : BLOCK + m + 16, :] = imag.astype(jnp.bfloat16)
        band_ref[1, m : m + 16, :] = (-imag).astype(jnp.bfloat16)
        band_ref[1, BLOCK + m : BLOCK + m + 16, :] = real.astype(jnp.bfloat16)


def place_of(group_ref):
    group = group_ref[0]
    return group // (CHIPS * CORES), group // CORES % CHIPS, group % CORES


def elimination(pairs, map_ref):
    total = map_ref.shape[0]
    label = lax.broadcasted_iota(jnp.int32, map_ref.shape, 0)
    incidence = jnp.where(label == pairs[1:2, :], 1.0, 0.0) - jnp.where(label == pairs[0:1, :], 1.0, 0.0)
    exact = incidence.astype(jnp.bfloat16)
    normal = lax.dot_general(exact, exact, (((1,), (1,)), ((), ())), preferred_element_type=jnp.float32)
    row = lax.broadcasted_iota(jnp.int32, (total, total), 0)
    column = lax.broadcasted_iota(jnp.int32, (total, total), 1)
    unit = jnp.where(row == column, 1.0, 0.0)
    table = jnp.concatenate([normal + RIDGE * unit, unit], axis=1)
    index = lax.broadcasted_iota(jnp.int32, table.shape, 0)
    def spread(k):
        return jnp.broadcast_to(table[:, k : k + 1], table.shape)

    spreads = [spread(k) for k in range(AHEAD)]
    for k in range(total):
        if k + AHEAD < total:
            spreads.append(spread(k + AHEAD))
        pivot = spreads.pop(0)
        scale = 1.0 / pivot[k : k + 1, :]

        def step(value):
            scaled = value[k : k + 1, :] * scale
            return jnp.where(index == k, scaled, value - pivot * scaled)

        table = step(table)
        spreads = [step(value) for value in spreads]
        yield
    map_ref[...] = jnp.dot(
        table[:, total:], incidence, precision=lax.Precision.HIGHEST, preferred_element_type=jnp.float32
    )


def filter_window(band_ref, a, windows):
    both = jnp.dot(band_ref[a, 0], windows[0], preferred_element_type=jnp.float32)
    both += jnp.dot(band_ref[a, 1], windows[1], preferred_element_type=jnp.float32)
    return both.astype(jnp.bfloat16)


def interior_kernel(
    taps_ref, pairs_ref, image_ref, out_ref, band_ref, edge_ref, map_ref, pairs, image, ordered, done, arrived, left
):
    _, local, rows, columns = image.shape
    blocks = rows // BLOCK
    inward = [pltpu.make_async_copy(image_ref.at[:, a], image.at[:, a], arrived.at[a]) for a in range(local)]
    inner = pl.ds(CORES, CORES * (blocks - 2))
    outward = [pltpu.make_async_copy(done.at[a], out_ref.at[inner, :, a], left.at[a]) for a in range(local)]
    listed = pltpu.make_async_copy(pairs_ref, pairs, arrived.at[local])
    listed.start()
    for copy in inward:
        copy.start()
    order = column_order(columns)
    fill_bands(taps_ref, band_ref.at[0], 0)
    listed.wait()
    solver = elimination(pairs[...], map_ref)

    def solve(steps):
        for _ in range(steps):
            next(solver, None)

    for a in range(1, local):
        fill_bands(taps_ref, band_ref.at[a], a)
        solve(SOLVER_STEPS)
    for a in range(local):
        inward[a].wait()
        for part in range(2):
            ordered[part] = jnp.dot(image[part, a], order, preferred_element_type=jnp.float32).astype(jnp.bfloat16)
            solve(SOLVER_STEPS)
            edge_ref[0, part, a] = ordered[part, :REST, :]
            edge_ref[1, part, a] = ordered[part, rows - REST :, :]
        for block in range(1, blocks - 1):
            window = pl.ds(block * BLOCK - HALO, 2 * BLOCK)
            both = filter_window(band_ref, a, [ordered[part, window, :] for part in range(2)])
            for core in range(CORES):
                for part in range(2):
                    start = part * BLOCK + core * CHUNK
                    done[a, (block - 1) * CORES + core, part] = both[start : start + CHUNK]
            solve(SOLVER_STEPS)
        outward[a].start()
    solve(1 + 8 * REST)
    for copy in outward:
        copy.wait()


def halo_kernel(odd_ref, image_ref, even_ref, odd_pairs_ref, arrived):
    rows = image_ref.shape[2]
    copies = []
    for start, out_ref in enumerate((even_ref, odd_pairs_ref)):
        at = pl.multiple_of(jnp.where(odd_ref[0] == start, rows - HALO, 0), HALO)
        copies.append(pltpu.make_async_copy(image_ref.at[:, :, pl.ds(at, HALO)], out_ref, arrived.at[start]))
        copies[-1].start()
    for copy in copies:
        copy.wait()


def edge_kernel(odd_ref, band_ref, edge_ref, odd_pairs_ref, even_ref, filled_ref, out_ref, done, left):
    del filled_ref
    local, columns = even_ref.shape[1], even_ref.shape[3]
    order = column_order(columns)
    copies = []
    received = []
    for halo_ref in (even_ref, odd_pairs_ref):
        flat = (halo_ref[part].reshape(local * HALO, columns) for part in range(2))
        received.append([jnp.dot(f, order, preferred_element_type=jnp.float32).astype(jnp.bfloat16) for f in flat])
    for e in range(2):
        halo = [jnp.where(odd_ref[0] == 1 - e, one, two) for one, two in zip(*received)]
        for a in range(local):
            windows = []
            for part in range(2):
                pieces = [halo[part][a * HALO : (a + 1) * HALO], edge_ref[e, part, a]]
                windows.append(jnp.concatenate(pieces if e == 0 else pieces[::-1], axis=0))
            both = filter_window(band_ref, a, windows)
            for core in range(CORES):
                for part in range(2):
                    start = part * BLOCK + core * CHUNK
                    done[e, a, core, part] = both[start : start + CHUNK]
            share = pl.ds(e * (out_ref.shape[0] - CORES), CORES)
            copies.append(pltpu.make_async_copy(done.at[e, a], out_ref.at[share, :, a], left.at[e, a]))
            copies[-1].start()
    for copy in copies:
        copy.wait()


def pair_kernel(pairs_ref, map_ref, got, out_ref, image, phase):
    groups, _, slots = got.shape[:3]

    def widen(g, slot):
        k = g * slots + slot
        real = got[g, 0, slot].astype(jnp.float32)
        imag = got[g, 1, slot].astype(jnp.float32)
        image[0, k] = real
        image[1, k] = imag
        image[2, k] = real - imag

    lane = lax.broadcasted_iota(jnp.int32, (8, 128), 1)
    low = lane < 64

    def fold(value):
        upper, lower = value[:8], value[8:]
        return jnp.where(low, upper, lower) + pltpu.roll(jnp.where(low, lower, upper), 64, 1)

    def plus(total, term):
        return term if total is None else total + term

    def one_reference(i):
        others = [pairs_ref[1, i * REACH + j] for j in range(REACH)]
        reals, imags, crossed = [None] * REACH, [None] * REACH, [None] * REACH
        for look in range(LOOK):
            for side in range(2):
                where = (pl.ds(look * 16, 16), pl.ds(side * 128, 128))
                a_re, a_im = (image[plane, i, where[0], where[1]] for plane in range(2))
                a_sum = a_re + a_im
                for j, k in enumerate(others):
                    b_re, b_im, b_less = (image[plane, k, where[0], where[1]] for plane in range(3))
                    reals[j] = plus(reals[j], a_re * b_re)
                    imags[j] = plus(imags[j], a_im * b_im)
                    crossed[j] = plus(crossed[j], a_sum * b_less)
        for j in range(REACH):
            re = fold(reals[j] + imags[j])
            im = fold(crossed[j] - reals[j] + imags[j])
            least = float(LOOK**4)
            ratio = im * lax.rsqrt(jnp.maximum(re * re + im * im, least))
            phase[pl.ds(pl.multiple_of((i * REACH + j) * 8, 8), 8), :] = ratio

    for g in range(groups):
        for slot in range(slots):
            widen(g, slot)
    lax.fori_loop(0, groups * slots, lambda i, carry: one_reference(i), None, unroll=16)

    table = map_ref[...]
    acqs, pairs = table.shape
    high = table.astype(jnp.bfloat16)
    rest = (table - high.astype(jnp.float32)).astype(jnp.bfloat16)
    stacked = jnp.concatenate([high, rest], axis=0)
    for t in range(8):
        value = phase[pl.ds(t, pairs, stride=8), :]
        v_high = value.astype(jnp.bfloat16)
        v_rest = (value - v_high.astype(jnp.float32)).astype(jnp.bfloat16)
        both = jnp.dot(stacked, v_high, preferred_element_type=jnp.float32)
        total = both[:acqs] + both[acqs:] + jnp.dot(high, v_rest, preferred_element_type=jnp.float32)
        out_ref[:, t * 128 : (t + 1) * 128] = total


def per_device(radar_stack, band_taps, pair_list):
    blocks_az = lax.axis_size("az")
    groups = lax.axis_size("acq")
    _, local, rows, columns = radar_stack.shape
    total_acq = groups * local
    odd = lax.axis_index("az") % 2
    meet = [[(i, i + 1) for i in range(start, blocks_az - 1, 2)] for start in range(2)]
    halo = pltpu.VMEM((2, local, HALO, columns), radar_stack.dtype)
    sent = pl.pallas_call(
        halo_kernel,
        in_specs=[SMEM, HBM],
        out_specs=[VMEM] * 2,
        out_shape=[halo] * 2,
        scratch_shapes=[pltpu.SemaphoreType.DMA((2,))],
        name="halo_rows",
    )(odd.reshape(1), pltpu.with_memory_space_constraint(radar_stack, pltpu.HBM))
    odd_pairs, even_pairs = (
        lax.ppermute(sent[start], "az", meet[start] + [(j, i) for i, j in meet[start]]) for start in (1, 0)
    )
    taps = jnp.pad(band_taps.astype(jnp.float32), ((0, 0), (0, 0), (0, 2 * BLOCK - band_taps.shape[2])))
    pairs = pair_list.T
    bf16, f32 = jnp.bfloat16, jnp.float32

    def settings(mib):
        return dict(
            compiler_params=pltpu.CompilerParams(vmem_limit_bytes=mib * MIB),
            cost_estimate=pl.CostEstimate(flops=2_000_000_000, bytes_accessed=9_000_000, transcendentals=0),
        )

    def in_hbm(value):
        return pltpu.with_memory_space_constraint(value, pltpu.HBM)

    inner = groups - 2 * CORES
    filtered, band, edge, inverse_map = pl.pallas_call(
        interior_kernel,
        in_specs=[VMEM, HBM, HBM],
        out_specs=[HBM, VMEM, VMEM, VMEM],
        out_shape=[
            pltpu.HBM((groups, 2, local, CHUNK, columns), bf16),
            pltpu.VMEM((local, 2, 2 * BLOCK, 2 * BLOCK), bf16),
            pltpu.VMEM((2, 2, local, REST, columns), bf16),
            jax.ShapeDtypeStruct((total_acq, pair_list.shape[0]), f32),
        ],
        scratch_shapes=[
            pltpu.VMEM(pairs.shape, pairs.dtype),
            pltpu.VMEM(radar_stack.shape, bf16),
            pltpu.VMEM((2, rows, columns), bf16),
            pltpu.VMEM((local, inner, 2, CHUNK, columns), bf16),
            pltpu.SemaphoreType.DMA((local + 1,)),
            pltpu.SemaphoreType.DMA((local,)),
        ],
        name="filter_interior",
        **settings(32),
    )(taps, in_hbm(pairs), in_hbm(radar_stack))
    filtered = pl.pallas_call(
        edge_kernel,
        in_specs=[SMEM] + [VMEM] * 4 + [HBM],
        out_specs=HBM,
        out_shape=pltpu.HBM(filtered.shape, bf16),
        input_output_aliases={5: 0},
        scratch_shapes=[
            pltpu.VMEM((2, local, CORES, 2, CHUNK, columns), bf16),
            pltpu.SemaphoreType.DMA((2, local)),
        ],
        name="filter_edges",
        **settings(24),
    )(odd.reshape(1), band, edge, odd_pairs, even_pairs, filtered)
    got = lax.all_to_all(filtered, "acq", 0, 0, tiled=True)
    return pl.pallas_call(
        pair_kernel,
        in_specs=[SMEM, VMEM, VMEM],
        out_specs=VMEM,
        out_shape=jax.ShapeDtypeStruct((total_acq, CHUNK // LOOK * columns // LOOK), f32),
        scratch_shapes=[
            pltpu.VMEM((3, total_acq, CHUNK, columns), f32),
            pltpu.VMEM((pair_list.shape[0] * 8, 128), f32),
        ],
        name="pairs_and_inversion",
        **settings(24),
    )(pairs, inverse_map, pltpu.with_memory_space_constraint(got, pltpu.VMEM))


def solution(mesh):
    return jax.shard_map(
        per_device,
        mesh=mesh,
        in_specs=(P(None, "acq", "az", None), P(None, "acq", None), P()),
        out_specs=P(None, ("az", "acq")),
        check_vma=False,
    )
```

```python
import jax
import jax.numpy as jnp
from jax import lax
from jax.experimental import pallas as pl
from jax.experimental.pallas import tpu as pltpu
from jax.sharding import PartitionSpec as P

LOOK = 4
REACH = 4
BLOCK = 128
CHUNK = 64
HALO = 64
REST = 2 * BLOCK - HALO
CORES = 2
AHEAD = 2
SOLVER_STEPS = 2
RIDGE = 1.0
MIB = 1 << 20
VMEM = pl.BlockSpec(memory_space=pltpu.VMEM)
SMEM = pl.BlockSpec(memory_space=pltpu.SMEM)
HBM = pl.BlockSpec(memory_space=pltpu.HBM)


def column_order(columns):
    source = lax.broadcasted_iota(jnp.int32, (columns, columns), 0)
    target = lax.broadcasted_iota(jnp.int32, (columns, columns), 1)
    looked = columns // LOOK
    wanted = (target % looked) * LOOK + target // looked
    return jnp.where(source == wanted, 1.0, 0.0).astype(jnp.bfloat16)


def fill_bands(taps_ref, band_ref, a):
    lines = [jnp.broadcast_to(taps_ref[part, a : a + 1, :], (8, 2 * BLOCK)) for part in range(2)]
    for m in range(0, BLOCK, 16):
        chunk, look = m // CHUNK, m % CHUNK // 16
        pieces = []
        for part in range(2):
            halves = [
                pltpu.roll(
                    lines[part], chunk * CHUNK + look + LOOK * half + 1, 1, stride=2 * LOOK, stride_axis=0
                )
                for half in range(2)
            ]
            pieces.append(jnp.concatenate(halves, axis=0))
        real, imag = pieces
        band_ref[0, m : m + 16, :] = real.astype(jnp.bfloat16)
        band_ref[0, BLOCK + m : BLOCK + m + 16, :] = imag.astype(jnp.bfloat16)
        band_ref[1, m : m + 16, :] = (-imag).astype(jnp.bfloat16)
        band_ref[1, BLOCK + m : BLOCK + m + 16, :] = real.astype(jnp.bfloat16)


def place_of(group_ref):
    group = group_ref[0]
    return group // (CHIPS * CORES), group // CORES % CHIPS, group % CORES


def elimination(pairs, map_ref):
    total = map_ref.shape[0]
    label = lax.broadcasted_iota(jnp.int32, map_ref.shape, 0)
    incidence = jnp.where(label == pairs[1:2, :], 1.0, 0.0) - jnp.where(label == pairs[0:1, :], 1.0, 0.0)
    exact = incidence.astype(jnp.bfloat16)
    normal = lax.dot_general(exact, exact, (((1,), (1,)), ((), ())), preferred_element_type=jnp.float32)
    row = lax.broadcasted_iota(jnp.int32, (total, total), 0)
    column = lax.broadcasted_iota(jnp.int32, (total, total), 1)
    unit = jnp.where(row == column, 1.0, 0.0)
    table = jnp.concatenate([normal + RIDGE * unit, unit], axis=1)
    index = lax.broadcasted_iota(jnp.int32, table.shape, 0)
    def spread(k):
        return jnp.broadcast_to(table[:, k : k + 1], table.shape)

    spreads = [spread(k) for k in range(AHEAD)]
    for k in range(total):
        if k + AHEAD < total:
            spreads.append(spread(k + AHEAD))
        pivot = spreads.pop(0)
        scale = 1.0 / pivot[k : k + 1, :]

        def step(value):
            scaled = value[k : k + 1, :] * scale
            return jnp.where(index == k, scaled, value - pivot * scaled)

        table = step(table)
        spreads = [step(value) for value in spreads]
        yield
    map_ref[...] = jnp.dot(
        table[:, total:], incidence, precision=lax.Precision.HIGHEST, preferred_element_type=jnp.float32
    )


def filter_window(band_ref, a, windows):
    both = jnp.dot(band_ref[a, 0], windows[0], preferred_element_type=jnp.float32)
    both += jnp.dot(band_ref[a, 1], windows[1], preferred_element_type=jnp.float32)
    return both.astype(jnp.bfloat16)


def interior_kernel(
    taps_ref, pairs_ref, image_ref, out_ref, band_ref, edge_ref, map_ref, pairs, image, ordered, done, arrived, left
):
    _, local, rows, columns = image.shape
    blocks = rows // BLOCK
    inward = [pltpu.make_async_copy(image_ref.at[:, a], image.at[:, a], arrived.at[a]) for a in range(local)]
    inner = pl.ds(CORES, CORES * (blocks - 2))
    outward = [pltpu.make_async_copy(done.at[a], out_ref.at[inner, :, a], left.at[a]) for a in range(local)]
    listed = pltpu.make_async_copy(pairs_ref, pairs, arrived.at[local])
    listed.start()
    for copy in inward:
        copy.start()
    order = column_order(columns)
    fill_bands(taps_ref, band_ref.at[0], 0)
    listed.wait()
    solver = elimination(pairs[...], map_ref)

    def solve(steps):
        for _ in range(steps):
            next(solver, None)

    for a in range(1, local):
        fill_bands(taps_ref, band_ref.at[a], a)
        solve(SOLVER_STEPS)
    for a in range(local):
        inward[a].wait()
        for part in range(2):
            ordered[part] = jnp.dot(image[part, a], order, preferred_element_type=jnp.float32).astype(jnp.bfloat16)
            solve(SOLVER_STEPS)
            edge_ref[0, part, a] = ordered[part, :REST, :]
            edge_ref[1, part, a] = ordered[part, rows - REST :, :]
        for block in range(1, blocks - 1):
            window = pl.ds(block * BLOCK - HALO, 2 * BLOCK)
            both = filter_window(band_ref, a, [ordered[part, window, :] for part in range(2)])
            for core in range(CORES):
                for part in range(2):
                    start = part * BLOCK + core * CHUNK
                    done[a, (block - 1) * CORES + core, part] = both[start : start + CHUNK]
            solve(SOLVER_STEPS)
        outward[a].start()
    solve(1 + 8 * REST)
    for copy in outward:
        copy.wait()


def edge_kernel(odd_ref, band_ref, edge_ref, even_ref, odd_pairs_ref, filled_ref, out_ref, done, left):
    del filled_ref
    local, columns = even_ref.shape[1], even_ref.shape[3]
    order = column_order(columns)
    copies = []
    received = []
    for halo_ref in (even_ref, odd_pairs_ref):
        flat = (halo_ref[part].reshape(local * HALO, columns) for part in range(2))
        received.append([jnp.dot(f, order, preferred_element_type=jnp.float32).astype(jnp.bfloat16) for f in flat])
    for e in range(2):
        halo = [jnp.where(odd_ref[0] == 1 - e, one, two) for one, two in zip(*received)]
        for a in range(local):
            windows = []
            for part in range(2):
                pieces = [halo[part][a * HALO : (a + 1) * HALO], edge_ref[e, part, a]]
                windows.append(jnp.concatenate(pieces if e == 0 else pieces[::-1], axis=0))
            both = filter_window(band_ref, a, windows)
            for core in range(CORES):
                for part in range(2):
                    start = part * BLOCK + core * CHUNK
                    done[e, a, core, part] = both[start : start + CHUNK]
            share = pl.ds(e * (out_ref.shape[0] - CORES), CORES)
            copies.append(pltpu.make_async_copy(done.at[e, a], out_ref.at[share, :, a], left.at[e, a]))
            copies[-1].start()
    for copy in copies:
        copy.wait()


def pair_kernel(pairs_ref, map_ref, got, out_ref, image, phase):
    groups, _, slots = got.shape[:3]

    def widen(g, slot):
        k = g * slots + slot
        real = got[g, 0, slot].astype(jnp.float32)
        imag = got[g, 1, slot].astype(jnp.float32)
        image[0, k] = real
        image[1, k] = imag
        image[2, k] = real - imag

    lane = lax.broadcasted_iota(jnp.int32, (8, 128), 1)
    low = lane < 64

    def fold(value):
        upper, lower = value[:8], value[8:]
        return jnp.where(low, upper, lower) + pltpu.roll(jnp.where(low, lower, upper), 64, 1)

    def plus(total, term):
        return term if total is None else total + term

    def one_reference(i):
        others = [pairs_ref[1, i * REACH + j] for j in range(REACH)]
        reals, imags, crossed = [None] * REACH, [None] * REACH, [None] * REACH
        for look in range(LOOK):
            for side in range(2):
                where = (pl.ds(look * 16, 16), pl.ds(side * 128, 128))
                a_re, a_im = (image[plane, i, where[0], where[1]] for plane in range(2))
                a_sum = a_re + a_im
                for j, k in enumerate(others):
                    b_re, b_im, b_less = (image[plane, k, where[0], where[1]] for plane in range(3))
                    reals[j] = plus(reals[j], a_re * b_re)
                    imags[j] = plus(imags[j], a_im * b_im)
                    crossed[j] = plus(crossed[j], a_sum * b_less)
        for j in range(REACH):
            re = fold(reals[j] + imags[j])
            im = fold(crossed[j] - reals[j] + imags[j])
            least = float(LOOK**4)
            ratio = im * lax.rsqrt(jnp.maximum(re * re + im * im, least))
            phase[pl.ds(pl.multiple_of((i * REACH + j) * 8, 8), 8), :] = ratio

    for g in range(groups):
        for slot in range(slots):
            widen(g, slot)
    lax.fori_loop(0, groups * slots, lambda i, carry: one_reference(i), None, unroll=32)

    table = map_ref[...]
    acqs, pairs = table.shape
    high = table.astype(jnp.bfloat16)
    rest = (table - high.astype(jnp.float32)).astype(jnp.bfloat16)
    stacked = jnp.concatenate([high, rest], axis=0)
    for t in range(8):
        value = phase[pl.ds(t, pairs, stride=8), :]
        v_high = value.astype(jnp.bfloat16)
        v_rest = (value - v_high.astype(jnp.float32)).astype(jnp.bfloat16)
        both = jnp.dot(stacked, v_high, preferred_element_type=jnp.float32)
        total = both[:acqs] + both[acqs:] + jnp.dot(high, v_rest, preferred_element_type=jnp.float32)
        out_ref[:, t * 128 : (t + 1) * 128] = total


def per_device(radar_stack, band_taps, pair_list):
    blocks_az = lax.axis_size("az")
    groups = lax.axis_size("acq")
    _, local, rows, columns = radar_stack.shape
    total_acq = groups * local
    odd = lax.axis_index("az") % 2
    meet = [[(i, i + 1) for i in range(start, blocks_az - 1, 2)] for start in range(2)]
    even_pairs, odd_pairs = (
        lax.ppermute(
            lax.dynamic_slice_in_dim(radar_stack, jnp.where(odd == start, rows - HALO, 0), HALO, 2),
            "az",
            ones + [(j, i) for i, j in ones],
        )
        for start, ones in enumerate(meet)
    )
    taps = jnp.pad(band_taps.astype(jnp.float32), ((0, 0), (0, 0), (0, 2 * BLOCK - band_taps.shape[2])))
    pairs = pair_list.T
    bf16, f32 = jnp.bfloat16, jnp.float32

    def settings(mib):
        return dict(
            compiler_params=pltpu.CompilerParams(vmem_limit_bytes=mib * MIB),
            cost_estimate=pl.CostEstimate(flops=2_000_000_000, bytes_accessed=9_000_000, transcendentals=0),
        )

    def in_hbm(value):
        return pltpu.with_memory_space_constraint(value, pltpu.HBM)

    inner = groups - 2 * CORES
    filtered, band, edge, inverse_map = pl.pallas_call(
        interior_kernel,
        in_specs=[VMEM, HBM, HBM],
        out_specs=[HBM, VMEM, VMEM, VMEM],
        out_shape=[
            pltpu.HBM((groups, 2, local, CHUNK, columns), bf16),
            pltpu.VMEM((local, 2, 2 * BLOCK, 2 * BLOCK), bf16),
            pltpu.VMEM((2, 2, local, REST, columns), bf16),
            jax.ShapeDtypeStruct((total_acq, pair_list.shape[0]), f32),
        ],
        scratch_shapes=[
            pltpu.VMEM(pairs.shape, pairs.dtype),
            pltpu.VMEM(radar_stack.shape, bf16),
            pltpu.VMEM((2, rows, columns), bf16),
            pltpu.VMEM((local, inner, 2, CHUNK, columns), bf16),
            pltpu.SemaphoreType.DMA((local + 1,)),
            pltpu.SemaphoreType.DMA((local,)),
        ],
        name="filter_interior",
        **settings(32),
    )(taps, in_hbm(pairs), in_hbm(radar_stack))
    filtered = pl.pallas_call(
        edge_kernel,
        in_specs=[SMEM] + [VMEM] * 4 + [HBM],
        out_specs=HBM,
        out_shape=pltpu.HBM(filtered.shape, bf16),
        input_output_aliases={5: 0},
        scratch_shapes=[
            pltpu.VMEM((2, local, CORES, 2, CHUNK, columns), bf16),
            pltpu.SemaphoreType.DMA((2, local)),
        ],
        name="filter_edges",
        **settings(24),
    )(odd.reshape(1), band, edge, even_pairs, odd_pairs, filtered)
    got = lax.all_to_all(filtered, "acq", 0, 0, tiled=True)
    return pl.pallas_call(
        pair_kernel,
        in_specs=[SMEM, VMEM, VMEM],
        out_specs=VMEM,
        out_shape=jax.ShapeDtypeStruct((total_acq, CHUNK // LOOK * columns // LOOK), f32),
        scratch_shapes=[
            pltpu.VMEM((3, total_acq, CHUNK, columns), f32),
            pltpu.VMEM((pair_list.shape[0] * 8, 128), f32),
        ],
        name="pairs_and_inversion",
        **settings(24),
    )(pairs, inverse_map, pltpu.with_memory_space_constraint(got, pltpu.VMEM))


def solution(mesh):
    return jax.shard_map(
        per_device,
        mesh=mesh,
        in_specs=(P(None, "acq", "az", None), P(None, "acq", None), P()),
        out_specs=P(None, ("az", "acq")),
        check_vma=False,
    )
```
